32 devices in a mesh: ens: 2 (over y), row: 4 (over x, core), col: 4 (over z).
Axes of the slice: x: 2, y: 2, z: 4, core: 2. Of those that a mesh axis runs over, the one named last changes fastest.
Arguments:
- left_proj: bfloat16 [128, 1024, 1024], P('ens', 'row', 'col'), parts along dimension 0, may hold values from -6 to 6
- right_proj: bfloat16 [128, 1024, 1024], P('ens', 'col', 'row'), parts along dimension 0, may hold values from -0.1875 to 0.1875
Outputs:
- update: float32 [128, 1024, 1024], P('ens', 'row', 'col'), parts along dimension 0
The draws below stay inside these ranges and needn't reach their ends.
There are 2 independent parts, one for each index of `ens`. The reference program is written for one: setup_inputs(seed, part) draws one part's arguments, and reference() takes and returns one part's arrays. A program takes and returns all parts, laid end to end along the dimension named above; each array names one. Nothing has to cross between parts.
All inputs are finite; a program needn't handle non-finite values.
Results may differ from the reference program's by a relative error of at most 0.0003.
Values may be sent and summed in bfloat16 or wider, within the bound.
No kernel may reach another device: no remote copies, remote signals or barrier semaphores. Data moves between devices by JAX's collectives and lax.ppermute only.
A program may use at most 192 MiB of HBM per device.

```python
import jax
import jax.numpy as jnp
from jax import lax

CH = 64
NTOK = 1024


def steps_of(stream_key, shape, pieces, low, largest):
    gain = 1.0
    for axis_at, blocks in pieces:
        heights = jax.random.uniform(jax.random.fold_in(jax.random.fold_in(stream_key, 6), axis_at), (blocks,), jnp.float32, low / len(pieces), largest / len(pieces))
        gain = gain * jnp.repeat(jnp.exp(heights), shape[axis_at] // blocks).reshape((-1,) + (1,) * (len(shape) - 1 - axis_at))
    return gain


def noise(stream_key, extent, deviation, reach, cuts=(), kind=jnp.bfloat16):
    loudness = steps_of(stream_key, extent, cuts, -0.22, 0.18) if cuts else 1.0
    values = jax.random.normal(stream_key, extent, jnp.float32) * deviation * loudness
    return jnp.minimum(jnp.maximum(values, -reach), reach).astype(kind)


def setup_inputs(seed: int = 0, part: int = 0) -> dict:
    key_list = jax.random.split(jax.random.key(seed), 3)
    own_keys = jax.random.split(jax.random.fold_in(key_list[2], part), 3)
    return {
        "left_proj": noise(own_keys[0], (CH, NTOK, NTOK), 1.0, 6.0, ((1, 4), (2, 4))),
        "right_proj": noise(own_keys[1], (CH, NTOK, NTOK), (NTOK ** -0.5), 0.1875, ((1, 4), (2, 4))),
    }


def one_channel(pair):
    left, right = pair
    return jnp.dot(left, right.T, preferred_element_type=jnp.float32)

def channel_norm(triangle):
    channel_mean = lax.optimization_barrier(jnp.mean(triangle, axis=0, keepdims=True))
    centered = triangle - channel_mean
    channel_var = lax.optimization_barrier(jnp.mean(centered * centered, axis=0, keepdims=True))
    return centered / jnp.sqrt(channel_var + 1e-05)

def reference(left_proj, right_proj):
    triangle = lax.map(one_channel, (left_proj, right_proj))
    return channel_norm(triangle)
```

```python
import functools

import jax
import jax.numpy as jnp
from jax import lax
from jax.experimental import pallas as pl
from jax.experimental.pallas import tpu as pltpu
from jax.sharding import PartitionSpec as P

EPS = 1e-5
HALF_SCALE = 16.0
VMEM = 48 * 1024 * 1024


def gathered(left_proj, right_proj):
    full_left = lax.all_gather(left_proj, "col", axis=2, tiled=True)
    full_right = lax.all_gather(right_proj, "row", axis=2, tiled=True)
    triangle = jnp.einsum("cik,cjk->cij", full_left, full_right, preferred_element_type=jnp.float32)
    channel_mean = jnp.mean(triangle, axis=0, keepdims=True)
    centered = triangle - channel_mean
    channel_var = jnp.mean(centered * centered, axis=0, keepdims=True)
    return centered / jnp.sqrt(channel_var + EPS)


def dot_nt(a, b):
    return lax.dot_general(a, b, (((1,), (1,)), ((), ())), preferred_element_type=jnp.float32)


def params():
    return pltpu.CompilerParams(vmem_limit_bytes=VMEM, dimension_semantics=("arbitrary",))


def tiles_kernel(step, choices, order, inner, *refs):
    *lefts, right, out = refs
    for c in range(step):
        acc, at = None, 0
        for turn, count in enumerate(choices):
            one = lefts[at][c]
            if count == 2:
                one = jnp.where(inner[0] == 1, one, lefts[at + 1][c])
            at += count
            term = dot_nt(one, right[order[turn], c])
            acc = term if acc is None else acc + term
        out[c] = acc


def tiles(order, inner, lefts, right, right_at, n):
    step = 4 if n % 4 == 0 and right_at % 4 == 0 and all(at % 4 == 0 for group in lefts for _, at in group) else 1
    flat = [pair for group in lefts for pair in group]
    rows, depth = flat[0][0].shape[1:]
    cols = right.shape[2]
    specs = [pl.BlockSpec((step, rows, depth), functools.partial(lambda off, c, *_: (off + c, 0, 0), at // step)) for _, at in flat]
    specs.append(pl.BlockSpec((4, step, cols, depth), lambda c, *_: (0, right_at // step + c, 0, 0)))
    return pl.pallas_call(
        functools.partial(tiles_kernel, step, tuple(len(group) for group in lefts)),
        grid_spec=pltpu.PrefetchScalarGridSpec(
            num_scalar_prefetch=2,
            grid=(n // step,),
            in_specs=specs,
            out_specs=pl.BlockSpec((step, rows, cols), lambda c, *_: (c, 0, 0)),
        ),
        out_shape=jax.ShapeDtypeStruct((n, rows, cols), jnp.float32),
        compiler_params=params(),
        cost_estimate=pl.CostEstimate(
            flops=8 * n * rows * cols * depth,
            bytes_accessed=n * ((len(flat) * rows + 4 * cols) * depth * 2 + rows * cols * 4),
            transcendentals=0,
        ),
        name="tiles",
    )(order, inner, *[array for array, _ in flat], right)


def norm_kernel(both, pairs, inner, *refs):
    *refs, out = refs
    shared, own, sent = refs[:both], refs[both : both + pairs], refs[both + pairs :]

    def write(parts):
        total = sum(jnp.sum(part[...], axis=0) for part in parts)
        channel_mean = total * (1.0 / out.shape[0])
        squares = 0.0
        for part in parts:
            centered = part[...] - channel_mean
            squares += jnp.sum(centered * centered, axis=0)
        factor = 1.0 / jnp.sqrt(squares * (1.0 / out.shape[0]) + EPS)
        at = 0
        for part in parts:
            n = part.shape[0]
            out[at : at + n] = (part[...] - channel_mean) * factor
            at += n

    @pl.when(inner[0] == 1)
    def _():
        write([*shared, *own])

    @pl.when(inner[0] != 1)
    def _():
        write([*shared, *sent])


def norm(inner, shared, own, sent):
    rows, cols = shared[0].shape[1:]
    channels = sum(part.shape[0] for part in [*shared, *own])
    step = 32
    spec = lambda part, used: pl.BlockSpec((part.shape[0], step, cols), lambda i, inner: (0, i * used(inner[0]), 0))
    specs = [spec(part, lambda flag: 1) for part in shared]
    specs += [spec(part, lambda flag: flag) for part in own]
    specs += [spec(part, lambda flag: 1 - flag) for part in sent]
    size = channels * rows * cols
    return pl.pallas_call(
        functools.partial(norm_kernel, len(shared), len(own)),
        grid_spec=pltpu.PrefetchScalarGridSpec(
            num_scalar_prefetch=1,
            grid=(rows // step,),
            in_specs=specs,
            out_specs=pl.BlockSpec((channels, step, cols), lambda i, inner: (0, i, 0)),
        ),
        out_shape=jax.ShapeDtypeStruct((channels, rows, cols), jnp.float32),
        compiler_params=params(),
        cost_estimate=pl.CostEstimate(flops=5 * size, bytes_accessed=8 * size, transcendentals=0),
        name="norm",
    )(inner, *shared, *own, *sent)


SWAP = [(0, 1), (1, 0), (2, 3), (3, 2)]
INWARD = [(0, 1), (3, 2)]
OUTWARD = [(1, 0), (2, 3)]
MIDDLE = [(1, 2), (2, 1)]


def after(block, *done):
    return lax.optimization_barrier((block, *done))[0] if done else block


class Slots:
    def __init__(self):
        self.ended = {}

    def held(self, k, block):
        return after(block, *self.ended.get(k - 2, []), *self.ended.get(k - 3, []))

    def go(self, k, block, pairs, *also):
        arrived = lax.ppermute(after(self.held(k, block), *also), "col", pairs)
        self.ended.setdefault(k, []).append(arrived)
        return arrived


def line(left, right):
    col = lax.axis_index("col")
    is_inner = (col == 1) | (col == 2)
    inner = is_inner.astype(jnp.int32).reshape(1)
    order = (col ^ jnp.where(is_inner, jnp.array([0, 1, 3, 2], jnp.int32), jnp.array([0, 1, 2, 3], jnp.int32))).astype(jnp.int32)
    quarter = left.shape[0] // 4
    half, eighth = 2 * quarter, quarter // 2

    slots = Slots()
    cut = lambda array, at, n: lax.slice_in_dim(array, at, at + n, axis=0)
    part = lambda k, array, at, n: cut(slots.held(k, array), at, n)
    rows_of = lambda block: lax.all_gather(block, "row", axis=0, tiled=False)
    na, nb, fa, fb = (0, quarter), (quarter, quarter), (half, quarter), (half + quarter, quarter)

    right_own = rows_of(right)
    first = cut(left, *na)
    p2_na, e_na = slots.go(0, first, MIDDLE), slots.go(0, first, SWAP)
    p2_nb, r_fa = slots.go(1, cut(left, *nb), MIDDLE), slots.go(1, cut(right, *fa), INWARD)
    p3_na, e_nb = slots.go(2, e_na, MIDDLE), slots.go(2, part(2, left, *nb), SWAP)
    q2_na = slots.go(2, p2_na, OUTWARD)
    p2_fa, r_fb = slots.go(3, part(3, left, *fa), MIDDLE), slots.go(3, part(3, right, *fb), INWARD)
    q2_nb = slots.go(3, p2_nb, OUTWARD, q2_na)
    p3_nb, e_fa = slots.go(4, e_nb, MIDDLE), slots.go(4, part(4, left, *fa), INWARD)
    q3_na = slots.go(4, p3_na, OUTWARD, q2_nb)
    p2_fb, e_fb = slots.go(5, part(5, left, *fb), MIDDLE, right_own), slots.go(5, part(5, left, *fb), INWARD)
    right_fa = rows_of(after(r_fa, p2_na, e_na))
    right_fb = rows_of(after(r_fb, p3_na, e_nb, q2_na))

    def near(at, e, p2, q2, p3, q3, *done):
        lefts = [[(after(left, *done), at)], [(e, 0)], [(p2, 0), (q2, 0)], [(p3, 0), (q3, 0)]]
        return tiles(order, inner, lefts, right_own, at, quarter)

    sizes = [eighth, eighth, eighth, eighth // 2, eighth // 2]
    starts = [sum(sizes[:k]) for k in range(len(sizes))]
    e_of = lambda at: (e_fa, at) if at < quarter else (e_fb, at - quarter)
    p2_of = lambda at: (p2_fa, at) if at < quarter else (p2_fb, at - quarter)
    right_of = lambda at: (right_fa, at) if at < quarter else (right_fb, at - quarter)
    lefts_of = lambda at, p3: [[(left, half + at)], [e_of(at)], [p2_of(at)], [(p3, 0)]]
    p3, shared, own, sent, payloads = [], [], [], [], []
    for k in range(len(sizes) + 2):
        if k >= 2:
            j = k - 2
            at, n = starts[j], sizes[j]
            tile = tiles(order, inner, lefts_of(at, p3[j]), *right_of(at), n) * HALF_SCALE
            if j == 0:
                offset = jnp.mean(tile, axis=0, keepdims=True).astype(jnp.float16)
            payload = (tile - offset.astype(jnp.float32)).astype(jnp.float16)
            if j == 0:
                payload = jnp.concatenate([payload, offset], axis=0)
            payloads.append(payload)
            ties = [last] if j != 1 else [last, shared[1]]
            if 2 <= j <= 3:
                ties.append(own[j - 2])
            last = arrived = lax.ppermute(after(payload, *ties), "col", OUTWARD)
            if j == 0:
                there = arrived[n:].astype(jnp.float32)
                arrived = arrived[:n]
                shared.append(near(quarter, e_nb, p2_nb, q2_nb, p3_nb, q3_nb, payload))
            sent.append((arrived.astype(jnp.float32) + there) * (1.0 / HALF_SCALE))
            own.append(tiles(order, inner, lefts_of(at, after(p3[j], payload)), right_own, half + at, n))
        if k < len(sizes):
            e, here = e_of(starts[k])
            block = cut(slots.held(6 + k, e), here, sizes[k])
            p3.append(slots.go(6 + k, block, MIDDLE, *payloads[-1:], *(shared[:1] if k == 1 else [])))
        if k == 0:
            q3_nb = last = slots.go(6, p3_nb, OUTWARD, q3_na)
            shared.append(near(0, e_na, p2_na, q2_na, p3_na, q3_na, p3_nb))
    return norm(inner, shared, own, sent)


def solution(mesh):
    placed = (P("ens", "row", "col"), P("ens", "col", "row"))
    per_device = line if mesh.shape["col"] == 4 and mesh.shape["row"] == 4 else gathered
    return jax.shard_map(
        per_device, mesh=mesh, in_specs=placed, out_specs=P("ens", "row", "col"), check_vma=False
    )
```

```python
import functools

import jax
import jax.numpy as jnp
from jax import lax
from jax.experimental import pallas as pl
from jax.experimental.pallas import tpu as pltpu
from jax.sharding import PartitionSpec as P

EPS = 1e-5
HALF_SCALE = 16.0


def gathered(left_proj, right_proj):
    full_left = lax.all_gather(left_proj, "col", axis=2, tiled=True)
    full_right = lax.all_gather(right_proj, "row", axis=2, tiled=True)
    triangle = jnp.einsum("cik,cjk->cij", full_left, full_right, preferred_element_type=jnp.float32)
    channel_mean = jnp.mean(triangle, axis=0, keepdims=True)
    centered = triangle - channel_mean
    channel_var = jnp.mean(centered * centered, axis=0, keepdims=True)
    return centered / jnp.sqrt(channel_var + EPS)


def dot_nt(a, b):
    return lax.dot_general(a, b, (((1,), (1,)), ((), ())), preferred_element_type=jnp.float32)


def params(limit):
    return pltpu.CompilerParams(vmem_limit_bytes=limit * 1024 * 1024, dimension_semantics=("arbitrary",))


def tiles_kernel(step, choices, order, inner, *refs):
    *lefts, right, out = refs
    for c in range(step):
        acc, at = None, 0
        for turn, count in enumerate(choices):
            one = lefts[at][c]
            if count == 2:
                one = jnp.where(inner[0] == 1, one, lefts[at + 1][c])
            at += count
            term = dot_nt(one, right[order[turn], c])
            acc = term if acc is None else acc + term
        out[c] = acc


def tiles(order, inner, lefts, right, right_at, n):
    step = 4 if n % 4 == 0 and right_at % 4 == 0 and all(at % 4 == 0 for group in lefts for _, at in group) else 1
    flat = [pair for group in lefts for pair in group]
    rows, depth = flat[0][0].shape[1:]
    cols = right.shape[2]
    specs = [pl.BlockSpec((step, rows, depth), functools.partial(lambda off, c, *_: (off + c, 0, 0), at // step)) for _, at in flat]
    specs.append(pl.BlockSpec((4, step, cols, depth), lambda c, *_: (0, right_at // step + c, 0, 0)))
    return pl.pallas_call(
        functools.partial(tiles_kernel, step, tuple(len(group) for group in lefts)),
        grid_spec=pltpu.PrefetchScalarGridSpec(
            num_scalar_prefetch=2,
            grid=(n // step,),
            in_specs=specs,
            out_specs=pl.BlockSpec((step, rows, cols), lambda c, *_: (c, 0, 0)),
        ),
        out_shape=jax.ShapeDtypeStruct((n, rows, cols), jnp.float32),
        compiler_params=params(32),
        cost_estimate=pl.CostEstimate(
            flops=8 * n * rows * cols * depth,
            bytes_accessed=n * ((len(flat) * rows + 4 * cols) * depth * 2 + rows * cols * 4),
            transcendentals=0,
        ),
        name="tiles",
    )(order, inner, *[array for array, _ in flat], right)


def norm_kernel(both, pairs, inner, *refs):
    *refs, out = refs
    shared, own, sent = refs[:both], refs[both : both + pairs], refs[both + pairs :]

    def write(parts):
        total = sum(jnp.sum(part[...], axis=0) for part in parts)
        channel_mean = total * (1.0 / out.shape[0])
        squares = 0.0
        for part in parts:
            centered = part[...] - channel_mean
            squares += jnp.sum(centered * centered, axis=0)
        factor = 1.0 / jnp.sqrt(squares * (1.0 / out.shape[0]) + EPS)
        at = 0
        for part in parts:
            n = part.shape[0]
            out[at : at + n] = (part[...] - channel_mean) * factor
            at += n

    @pl.when(inner[0] == 1)
    def _():
        write([*shared, *own])

    @pl.when(inner[0] != 1)
    def _():
        write([*shared, *sent])


def norm(inner, shared, own, sent):
    rows, cols = shared[0].shape[1:]
    channels = sum(part.shape[0] for part in [*shared, *own])
    step = 32
    spec = lambda part, used: pl.BlockSpec((part.shape[0], step, cols), lambda i, inner: (0, i * used(inner[0]), 0))
    specs = [spec(part, lambda flag: 1) for part in shared]
    specs += [spec(part, lambda flag: flag) for part in own]
    specs += [spec(part, lambda flag: 1 - flag) for part in sent]
    size = channels * rows * cols
    return pl.pallas_call(
        functools.partial(norm_kernel, len(shared), len(own)),
        grid_spec=pltpu.PrefetchScalarGridSpec(
            num_scalar_prefetch=1,
            grid=(rows // step,),
            in_specs=specs,
            out_specs=pl.BlockSpec((channels, step, cols), lambda i, inner: (0, i, 0)),
        ),
        out_shape=jax.ShapeDtypeStruct((channels, rows, cols), jnp.float32),
        compiler_params=params(20),
        cost_estimate=pl.CostEstimate(flops=5 * size, bytes_accessed=8 * size, transcendentals=0),
        name="norm",
    )(inner, *shared, *own, *sent)


SWAP = [(0, 1), (1, 0), (2, 3), (3, 2)]
INWARD = [(0, 1), (3, 2)]
OUTWARD = [(1, 0), (2, 3)]
MIDDLE = [(1, 2), (2, 1)]


def after(block, *done):
    return lax.optimization_barrier((block, *done))[0] if done else block


def find(parts, at):
    first, array = [part for part in parts if part[0] <= at][-1]
    return array, at - first


def line(left, right):
    col = lax.axis_index("col")
    is_inner = (col == 1) | (col == 2)
    inner = is_inner.astype(jnp.int32).reshape(1)
    order = (col ^ jnp.where(is_inner, jnp.array([0, 1, 3, 2], jnp.int32), jnp.array([0, 1, 2, 3], jnp.int32))).astype(jnp.int32)
    half, quarter, unit = left.shape[0] // 2, left.shape[0] // 4, left.shape[0] // 16

    cut = lambda array, at, n: lax.slice_in_dim(array, at, at + n, axis=0)
    go = lambda block, pairs: lax.ppermute(block, "col", pairs)
    rows_of = lambda block: lax.all_gather(block, "row", axis=0, tiled=False)

    right_own = rows_of(right)
    first = cut(left, 0, half)
    e_n, p2_n = go(first, SWAP), go(first, MIDDLE)
    left_on, right_on = after(left, first), after(right, first)
    second, f0, f1 = cut(left_on, half, half), cut(left_on, half, unit), cut(left_on, half + unit, half - unit)
    fa, fb = cut(right_on, half, 3 * unit), cut(right_on, half + 3 * unit, 5 * unit)
    ended = (e_n, p2_n, second, f0, f1, fa, fb)

    p3_n = go(after(e_n, *ended), MIDDLE)
    r_fa, r_fb = go(after(fa, *ended), INWARD), go(after(fb, *ended), INWARD)
    q2_n = go(after(p2_n, *ended), OUTWARD)
    ended = (p3_n, r_fa, r_fb, q2_n)

    right_f = [(0, rows_of(after(r_fa, *ended))), (3 * unit, rows_of(after(r_fb, *ended)))]
    p2_f = go(after(second, *ended), MIDDLE)
    e_f = [(0, go(after(f0, *ended), INWARD)), (unit, go(after(f1, *ended), INWARD))]
    q3_na = go(cut(after(p3_n, *ended), 0, quarter), OUTWARD)
    q3_nb = go(cut(after(p3_n, *ended, q3_na), quarter, quarter), OUTWARD)

    def near(at, q3, *done):
        lefts = [[(after(left, *done), at)], [(e_n, at)], [(p2_n, at), (q2_n, at)], [(p3_n, at), (q3, 0)]]
        return tiles(order, inner, lefts, right_own, at, quarter)

    near_a = near(0, q3_na)
    ended = (p2_f, e_f[0][1], e_f[1][1], q3_nb, near_a)

    sizes = [unit, 2 * unit, 2 * unit, 2 * unit, unit]
    starts = [sum(sizes[:k]) for k in range(len(sizes))]
    lefts_of = lambda at, p3: [[(left, half + at)], [find(e_f, at)], [(p2_f, at)], [(p3, 0)]]
    held = [(first, after(array, *ended)) for first, array in e_f]
    p3 = []
    for at, n in zip(starts, sizes):
        array, here = find(held, at)
        p3.append(go(cut(array, here, n) if n < array.shape[0] else array, MIDDLE))
    own, sent, payloads, outward = [], [], [], [None, q3_nb]
    for j, (at, n) in enumerate(zip(starts, sizes)):
        tile = tiles(order, inner, lefts_of(at, after(p3[j], *payloads[-1:], *outward[j : j + 1][: j - 1 if j > 1 else 0])), *find(right_f, at), n) * HALF_SCALE
        if j == 0:
            offset = jnp.mean(tile, axis=0, keepdims=True).astype(jnp.float16)
        payload = (after(tile, *payloads[-1:]) - offset.astype(jnp.float32)).astype(jnp.float16)
        payloads.append(payload)
        if j == 0:
            payload = jnp.concatenate([payload, offset], axis=0)
        if j == 1:
            near_b = near(quarter, q3_nb, payload)
        ties = outward[j : j + 1] if j else []
        if j == 3:
            ties += [near_b, own[0]]
        if j == 4:
            ties += own[1:3]
        arrived = go(after(payload, *ties, *sent[: max(j - 1, 0)]), OUTWARD)
        outward.append(arrived)
        if j == 0:
            there = arrived[n:].astype(jnp.float32)
            arrived = arrived[:n]
        sent.append((arrived.astype(jnp.float32) + there) * (1.0 / HALF_SCALE))
        own.append(tiles(order, inner, lefts_of(at, after(p3[j], payload)), right_own, half + at, n))
    return norm(inner, [near_a, near_b], own, sent)


def solution(mesh):
    placed = (P("ens", "row", "col"), P("ens", "col", "row"))
    per_device = line if mesh.shape["col"] == 4 and mesh.shape["row"] == 4 else gathered
    return jax.shard_map(
        per_device, mesh=mesh, in_specs=placed, out_specs=P("ens", "row", "col"), check_vma=False
    )
```

```python
import functools

import jax
import jax.numpy as jnp
from jax import lax
from jax.experimental import pallas as pl
from jax.experimental.pallas import tpu as pltpu
from jax.sharding import PartitionSpec as P

EPS = 1e-5
HALF_SCALE = 16.0


def gathered(left_proj, right_proj):
    full_left = lax.all_gather(left_proj, "col", axis=2, tiled=True)
    full_right = lax.all_gather(right_proj, "row", axis=2, tiled=True)
    triangle = jnp.einsum("cik,cjk->cij", full_left, full_right, preferred_element_type=jnp.float32)
    channel_mean = jnp.mean(triangle, axis=0, keepdims=True)
    centered = triangle - channel_mean
    channel_var = jnp.mean(centered * centered, axis=0, keepdims=True)
    return centered / jnp.sqrt(channel_var + EPS)


def dot_nt(a, b):
    return lax.dot_general(a, b, (((1,), (1,)), ((), ())), preferred_element_type=jnp.float32)


def params(limit):
    return pltpu.CompilerParams(vmem_limit_bytes=limit * 1024 * 1024, dimension_semantics=("arbitrary",))


def tiles_kernel(step, scale, groups, order, inner, *refs):
    *lefts, right, out = refs
    for c in range(step):
        acc, at = None, 0
        for turn, begins in enumerate(groups):
            one = lefts[at][c]
            for k, begin in enumerate(begins[1:], 1):
                other = inner[0] != 1 if begin is None else pl.program_id(0) >= begin
                one = jnp.where(other, lefts[at + k][c], one)
            at += len(begins)
            term = dot_nt(one, right[order[turn], c])
            acc = term if acc is None else acc + term
        out[c] = acc if scale == 1.0 else acc * scale


def tiles(order, inner, lefts, right, right_at, n, scale=1.0):
    step = 4
    arrays, specs, groups = [], [], []
    rows, depth = lefts[0][0][0].shape[1:]
    cols = right.shape[2]

    def block(index):
        specs.append(pl.BlockSpec((step, rows, depth), lambda c, order, inner: (index(c, inner[0]), 0, 0)))

    for group in lefts:
        if isinstance(group[0], tuple):
            (array, at), *outer = group
            arrays.append(array)
            if not outer:
                block(lambda c, flag, at=at // step: at + c)
            else:
                arrays.append(outer[0][0])
                block(lambda c, flag, at=at // step: at + c * flag)
                block(lambda c, flag, at=outer[0][1] // step: at + c * (1 - flag))
            groups.append((0, None)[: len(group)])
        else:
            begins, begin = [], 0
            for array in group:
                count = array.shape[0] // step
                block(lambda c, flag, begin=begin, count=count: jnp.clip(c - begin, 0, count - 1))
                arrays.append(array)
                begins.append(begin)
                begin += count
            groups.append(tuple(begins))
    specs.append(pl.BlockSpec((4, step, cols, depth), lambda c, *_: (0, right_at // step + c, 0, 0)))
    return pl.pallas_call(
        functools.partial(tiles_kernel, step, scale, tuple(groups)),
        grid_spec=pltpu.PrefetchScalarGridSpec(
            num_scalar_prefetch=2,
            grid=(n // step,),
            in_specs=specs,
            out_specs=pl.BlockSpec((step, rows, cols), lambda c, *_: (c, 0, 0)),
        ),
        out_shape=jax.ShapeDtypeStruct((n, rows, cols), jnp.float32),
        compiler_params=params(32),
        cost_estimate=pl.CostEstimate(
            flops=8 * n * rows * cols * depth,
            bytes_accessed=n * (4 * (rows + cols) * depth * 2 + rows * cols * 4),
            transcendentals=0,
        ),
        name="tiles",
    )(order, inner, *arrays, right)


def norm_kernel(both, mine, inner, offset, first, second, *refs):
    *refs, out = refs
    shared, own, sent = refs[:both], refs[both : both + mine], refs[both + mine :]
    share = 1.0 / out.shape[0]

    def write(parts):
        sums, squares = first[...], second[...]
        for part in parts:
            for c in range(part.shape[0]):
                apart = part[c] - offset[...]
                sums += apart
                squares += apart * apart
        shift = sums * share
        channel_var = jnp.maximum(squares * share - shift * shift, 0.0)
        channel_mean = offset[...] + shift
        factor = 1.0 / jnp.sqrt(channel_var + EPS)
        at = 0
        for part in [*shared, *parts]:
            for c in range(part.shape[0]):
                out[at + c] = (part[c] - channel_mean) * factor
            at += part.shape[0]

    @pl.when(inner[0] == 1)
    def _():
        write(own)

    @pl.when(inner[0] != 1)
    def _():
        write(sent)


def norm(inner, stats, shared, own, sent):
    rows, cols = shared[0].shape[1:]
    channels = sum(part.shape[0] for part in [*shared, *own])
    step = 32
    spec = lambda part, used: pl.BlockSpec((part.shape[0], step, cols), lambda i, inner: (0, i * used(inner[0]), 0))
    specs = [pl.BlockSpec((step, cols), lambda i, inner: (i, 0)) for _ in stats]
    specs += [spec(part, lambda flag: 1) for part in shared]
    specs += [spec(part, lambda flag: flag) for part in own]
    specs += [spec(part, lambda flag: 1 - flag) for part in sent]
    size = channels * rows * cols
    return pl.pallas_call(
        functools.partial(norm_kernel, len(shared), len(own)),
        grid_spec=pltpu.PrefetchScalarGridSpec(
            num_scalar_prefetch=1,
            grid=(rows // step,),
            in_specs=specs,
            out_specs=pl.BlockSpec((channels, step, cols), lambda i, inner: (0, i, 0)),
        ),
        out_shape=jax.ShapeDtypeStruct((channels, rows, cols), jnp.float32),
        compiler_params=params(44),
        cost_estimate=pl.CostEstimate(flops=5 * size, bytes_accessed=8 * size, transcendentals=0),
        name="norm",
    )(inner, *stats, *shared, *own, *sent)


SWAP = [(0, 1), (1, 0), (2, 3), (3, 2)]
INWARD = [(0, 1), (3, 2)]
OUTWARD = [(1, 0), (2, 3)]
MIDDLE = [(1, 2), (2, 1)]


def after(block, *done):
    return lax.optimization_barrier((block, *done))[0] if done else block


def line(left, right):
    col = lax.axis_index("col")
    is_inner = (col == 1) | (col == 2)
    inner = is_inner.astype(jnp.int32).reshape(1)
    order = (col ^ jnp.where(is_inner, jnp.array([0, 1, 3, 2], jnp.int32), jnp.array([0, 1, 2, 3], jnp.int32))).astype(jnp.int32)
    unit = left.shape[0] // 16
    near_n, far_n = 8 * unit, 8 * unit
    near_sizes, sizes = [4 * unit, 4 * unit], [2 * unit] * 4

    cut = lambda array, at, n: lax.slice_in_dim(array, at, at + n, axis=0)
    pieces = lambda array, at, counts: [cut(array, at + sum(counts[:k]), n) for k, n in enumerate(counts)]
    go = lambda block, pairs: lax.ppermute(block, "col", pairs)
    rows_of = lambda block: lax.all_gather(block, "row", axis=0, tiled=False)

    right_own = rows_of(right)
    first = cut(left, 0, near_n)
    e_n, p2_n = go(first, SWAP), go(first, MIDDLE)
    left_on = after(left, first)
    second, *split = cut(left_on, near_n, far_n), *pieces(left_on, near_n, [sizes[0], far_n - sizes[0]])
    third = cut(after(right, first), near_n, far_n)
    ended = (e_n, second, *split, third)

    p3_n = go(after(e_n, *ended), MIDDLE)
    r_f = go(after(third, *ended, p2_n), INWARD)
    q2_n = go(after(p2_n, *ended), OUTWARD)
    ended = (p3_n, q2_n)

    right_f = rows_of(after(r_f, *ended))
    p2_f = go(after(second, *ended), MIDDLE)
    e_f = [go(after(split[0], *ended), INWARD)]
    e_f.append(go(after(split[1], *ended, e_f[0]), INWARD))
    q3_na = go(cut(after(p3_n, *ended), 0, near_sizes[0]), OUTWARD)
    q3_nb = go(cut(after(p3_n, *ended, q3_na, right_own), *near_sizes), OUTWARD)

    def near(at, q3, n, *done):
        blocks = [[(after(left, *done), at)], [(e_n, at)], [(p2_n, at), (q2_n, at)], [(p3_n, at), (q3, 0)]]
        return tiles(order, inner, blocks, right_own, at, n)

    def stats_of(offset, block, first, second):
        apart = block - offset
        return first + jnp.sum(apart, axis=0), second + jnp.sum(apart * apart, axis=0)

    near_a = near(0, q3_na, near_sizes[0])
    offset = jnp.mean(near_a, axis=0)
    there = (offset * HALF_SCALE).astype(jnp.float16)
    here = go(there, INWARD)
    stats = stats_of(offset, near_a, 0.0, 0.0)
    p3 = [go(after(e_f[0], there), MIDDLE)]
    ended = (p2_f, *e_f)
    p3 += [go(block, MIDDLE) for block in pieces(after(e_f[1], *ended), 0, sizes[1:])]
    sent, payloads, returned, at = [], [], [], 0
    for j, n in enumerate(sizes):
        waits = [*payloads[-1:], *returned[: max(j - 1, 0)], *([near_b] if j == 1 else []), *([q3_nb] if j == 0 else [])]
        blocks = [[(second, at)], [(e_f[1], at - sizes[0]) if j else (e_f[0], 0)], [(p2_f, at)], [(after(p3[j], *waits), 0)]]
        tile = tiles(order, inner, blocks, right_f, at, n, HALF_SCALE)
        payload = (tile - here.astype(jnp.float32)).astype(jnp.float16)
        payloads.append(payload)
        if j == 0:
            near_b = near(near_sizes[0], q3_nb, near_sizes[1], payload)
            stats = stats_of(offset, near_b, *stats)
        ties = [(), (near_b, *returned), (*stats, *returned[1:]), returned[2:]][j]
        arrived = go(after(payload, *ties), OUTWARD)
        returned.append(arrived)
        back = after(arrived, *sent[-1:])
        sent.append((back.astype(jnp.float32) + there.astype(jnp.float32)) * (1.0 / HALF_SCALE))
        at += n
    own = tiles(order, inner, [[(after(second, payloads[-1]), 0)], e_f, [(p2_f, 0)], p3], right_own, near_n, far_n)
    return norm(inner, (offset, *stats), [near_a, near_b], [own], sent)


def solution(mesh):
    placed = (P("ens", "row", "col"), P("ens", "col", "row"))
    per_device = line if mesh.shape["col"] == 4 and mesh.shape["row"] == 4 else gathered
    return jax.shard_map(
        per_device, mesh=mesh, in_specs=placed, out_specs=P("ens", "row", "col"), check_vma=False
    )
```

```python
import functools

import jax
import jax.numpy as jnp
from jax import lax
from jax.experimental import pallas as pl
from jax.experimental.pallas import tpu as pltpu
from jax.sharding import PartitionSpec as P

EPS = 1e-5
HALF_SCALE = 16.0


def gathered(left_proj, right_proj):
    full_left = lax.all_gather(left_proj, "col", axis=2, tiled=True)
    full_right = lax.all_gather(right_proj, "row", axis=2, tiled=True)
    triangle = jnp.einsum("cik,cjk->cij", full_left, full_right, preferred_element_type=jnp.float32)
    channel_mean = jnp.mean(triangle, axis=0, keepdims=True)
    centered = triangle - channel_mean
    channel_var = jnp.mean(centered * centered, axis=0, keepdims=True)
    return centered / jnp.sqrt(channel_var + EPS)


def dot_nt(a, b):
    return lax.dot_general(a, b, (((1,), (1,)), ((), ())), preferred_element_type=jnp.float32)


def params(limit):
    return pltpu.CompilerParams(vmem_limit_bytes=limit * 1024 * 1024, dimension_semantics=("arbitrary",))


def tiles_kernel(step, scale, groups, order, inner, *refs):
    *lefts, right, out = refs
    for c in range(step):
        acc, at = None, 0
        for turn, begins in enumerate(groups):
            one = lefts[at][c]
            for k, begin in enumerate(begins[1:], 1):
                other = inner[0] != 1 if begin is None else pl.program_id(0) >= begin
                one = jnp.where(other, lefts[at + k][c], one)
            at += len(begins)
            term = dot_nt(one, right[order[turn], c])
            acc = term if acc is None else acc + term
        out[c] = acc if scale == 1.0 else acc * scale


def tiles(order, inner, lefts, right, right_at, n, scale=1.0):
    step = 4
    arrays, specs, groups = [], [], []
    rows, depth = lefts[0][0][0].shape[1:]
    cols = right.shape[2]

    def block(index):
        specs.append(pl.BlockSpec((step, rows, depth), lambda c, order, inner: (index(c, inner[0]), 0, 0)))

    for group in lefts:
        if isinstance(group[0], tuple):
            (array, at), *outer = group
            arrays.append(array)
            if not outer:
                block(lambda c, flag, at=at // step: at + c)
            else:
                arrays.append(outer[0][0])
                block(lambda c, flag, at=at // step: at + c * flag)
                block(lambda c, flag, at=outer[0][1] // step: at + c * (1 - flag))
            groups.append((0, None)[: len(group)])
        else:
            begins, begin = [], 0
            for array in group:
                count = array.shape[0] // step
                block(lambda c, flag, begin=begin, count=count: jnp.clip(c - begin, 0, count - 1))
                arrays.append(array)
                begins.append(begin)
                begin += count
            groups.append(tuple(begins))
    specs.append(pl.BlockSpec((4, step, cols, depth), lambda c, *_: (0, right_at // step + c, 0, 0)))
    return pl.pallas_call(
        functools.partial(tiles_kernel, step, scale, tuple(groups)),
        grid_spec=pltpu.PrefetchScalarGridSpec(
            num_scalar_prefetch=2,
            grid=(n // step,),
            in_specs=specs,
            out_specs=pl.BlockSpec((step, rows, cols), lambda c, *_: (c, 0, 0)),
        ),
        out_shape=jax.ShapeDtypeStruct((n, rows, cols), jnp.float32),
        compiler_params=params(48),
        cost_estimate=pl.CostEstimate(
            flops=8 * n * rows * cols * depth,
            bytes_accessed=n * (4 * (rows + cols) * depth * 2 + rows * cols * 4),
            transcendentals=0,
        ),
        name="tiles",
    )(order, inner, *arrays, right)


def norm_kernel(both, mine, inner, offset, first, second, *refs):
    *refs, out = refs
    shared, own, sent = refs[:both], refs[both : both + mine], refs[both + mine :]
    share = 1.0 / out.shape[0]

    def write(parts):
        sums, squares = first[...], second[...]
        for part in parts:
            for c in range(part.shape[0]):
                apart = part[c] - offset[...]
                sums += apart
                squares += apart * apart
        shift = sums * share
        channel_var = jnp.maximum(squares * share - shift * shift, 0.0)
        channel_mean = offset[...] + shift
        factor = 1.0 / jnp.sqrt(channel_var + EPS)
        at = 0
        for part in [*shared, *parts]:
            for c in range(part.shape[0]):
                out[at + c] = (part[c] - channel_mean) * factor
            at += part.shape[0]

    @pl.when(inner[0] == 1)
    def _():
        write(own)

    @pl.when(inner[0] != 1)
    def _():
        write(sent)


def norm(inner, stats, shared, own, sent):
    rows, cols = shared[0].shape[1:]
    channels = sum(part.shape[0] for part in [*shared, *own])
    step = 32
    spec = lambda part, used: pl.BlockSpec((part.shape[0], step, cols), lambda i, inner: (0, i * used(inner[0]), 0))
    specs = [pl.BlockSpec((step, cols), lambda i, inner: (i, 0)) for _ in stats]
    specs += [spec(part, lambda flag: 1) for part in shared]
    specs += [spec(part, lambda flag: flag) for part in own]
    specs += [spec(part, lambda flag: 1 - flag) for part in sent]
    size = channels * rows * cols
    return pl.pallas_call(
        functools.partial(norm_kernel, len(shared), len(own)),
        grid_spec=pltpu.PrefetchScalarGridSpec(
            num_scalar_prefetch=1,
            grid=(rows // step,),
            in_specs=specs,
            out_specs=pl.BlockSpec((channels, step, cols), lambda i, inner: (0, i, 0)),
        ),
        out_shape=jax.ShapeDtypeStruct((channels, rows, cols), jnp.float32),
        compiler_params=params(44),
        cost_estimate=pl.CostEstimate(flops=5 * size, bytes_accessed=8 * size, transcendentals=0),
        name="norm",
    )(inner, *stats, *shared, *own, *sent)


SWAP = [(0, 1), (1, 0), (2, 3), (3, 2)]
INWARD = [(0, 1), (3, 2)]
OUTWARD = [(1, 0), (2, 3)]
MIDDLE = [(1, 2), (2, 1)]


def after(block, *done):
    return lax.optimization_barrier((block, *done))[0] if done else block


def line(left, right):
    col = lax.axis_index("col")
    is_inner = (col == 1) | (col == 2)
    inner = is_inner.astype(jnp.int32).reshape(1)
    order = (col ^ jnp.where(is_inner, jnp.array([0, 1, 3, 2], jnp.int32), jnp.array([0, 1, 2, 3], jnp.int32))).astype(jnp.int32)
    unit = left.shape[0] // 16
    near_n, far_n = 8 * unit, 8 * unit
    near_sizes, sizes = [4 * unit, 4 * unit], [2 * unit] * 4

    cut = lambda array, at, n: lax.slice_in_dim(array, at, at + n, axis=0)
    pieces = lambda array, at, counts: [cut(array, at + sum(counts[:k]), n) for k, n in enumerate(counts)]
    go = lambda block, pairs: lax.ppermute(block, "col", pairs)
    rows_of = lambda block: lax.all_gather(block, "row", axis=0, tiled=False)

    right_own = rows_of(right)
    first = cut(left, 0, near_n)
    e_n, p2_n = go(first, SWAP), go(first, MIDDLE)
    left_on = after(left, first)
    second, *split = cut(left_on, near_n, far_n), *pieces(left_on, near_n, [sizes[0], far_n - sizes[0]])
    third = cut(after(right, first), near_n, far_n)
    ended = (e_n, second, *split, third)

    p3_n = go(after(e_n, *ended), MIDDLE)
    r_f = go(after(third, *ended, p2_n), INWARD)
    q2_n = go(after(p2_n, *ended), OUTWARD)
    ended = (p3_n, q2_n)

    right_f = rows_of(after(r_f, *ended))
    p2_f = go(after(second, *ended), MIDDLE)
    e_f = [go(after(split[0], *ended), INWARD)]
    e_f.append(go(after(split[1], *ended, e_f[0]), INWARD))
    q3_na = go(cut(after(p3_n, *ended), 0, near_sizes[0]), OUTWARD)
    q3_nb = go(cut(after(p3_n, *ended, q3_na, right_own), *near_sizes), OUTWARD)

    def near(at, q3, n, *done):
        blocks = [[(after(left, *done), at)], [(e_n, at)], [(p2_n, at), (q2_n, at)], [(p3_n, at), (q3, 0)]]
        return tiles(order, inner, blocks, right_own, at, n)

    def stats_of(offset, block, first, second):
        apart = block - offset
        return first + jnp.sum(apart, axis=0), second + jnp.sum(apart * apart, axis=0)

    near_a = near(0, q3_na, near_sizes[0])
    offset = jnp.mean(near_a, axis=0)
    there = (offset * HALF_SCALE).astype(jnp.float16)
    here = go(there, INWARD)
    stats = stats_of(offset, near_a, 0.0, 0.0)
    p3 = [go(after(e_f[0], there), MIDDLE)]
    ended = (p2_f, *e_f)
    p3 += [go(block, MIDDLE) for block in pieces(after(e_f[1], *ended), 0, sizes[1:])]
    sent, payloads, returned, at = [], [], [], 0
    for j, n in enumerate(sizes):
        waits = [*payloads[-1:], *returned[: max(j - 1, 0)], *([near_b] if j == 1 else []), *([q3_nb] if j == 0 else [])]
        blocks = [[(second, at)], [(e_f[1], at - sizes[0]) if j else (e_f[0], 0)], [(p2_f, at)], [(after(p3[j], *waits), 0)]]
        tile = tiles(order, inner, blocks, right_f, at, n, HALF_SCALE)
        payload = (tile - here.astype(jnp.float32)).astype(jnp.float16)
        payloads.append(payload)
        if j == 0:
            near_b = near(near_sizes[0], q3_nb, near_sizes[1], payload)
            stats = stats_of(offset, near_b, *stats)
        ties = [(), (near_b, *returned), (*stats, *returned[1:]), returned[2:]][j]
        arrived = go(after(payload, *ties), OUTWARD)
        returned.append(arrived)
        back = after(arrived, *sent[-1:])
        sent.append((back.astype(jnp.float32) + there.astype(jnp.float32)) * (1.0 / HALF_SCALE))
        at += n
    own = tiles(order, inner, [[(after(second, payloads[-1]), 0)], e_f, [(p2_f, 0)], p3], right_own, near_n, far_n)
    return norm(inner, (offset, *stats), [near_a, near_b], [own], sent)


def solution(mesh):
    placed = (P("ens", "row", "col"), P("ens", "col", "row"))
    per_device = line if mesh.shape["col"] == 4 and mesh.shape["row"] == 4 else gathered
    return jax.shard_map(
        per_device, mesh=mesh, in_specs=placed, out_specs=P("ens", "row", "col"), check_vma=False
    )
```

```python
import functools

import jax
import jax.numpy as jnp
from jax import lax
from jax.experimental import pallas as pl
from jax.experimental.pallas import tpu as pltpu
from jax.sharding import PartitionSpec as P

EPS = 1e-5
HALF_SCALE = 16.0
HALF_REACH = 32768.0


def gathered(left_proj, right_proj):
    full_left = lax.all_gather(left_proj, "col", axis=2, tiled=True)
    full_right = lax.all_gather(right_proj, "row", axis=2, tiled=True)
    triangle = jnp.einsum("cik,cjk->cij", full_left, full_right, preferred_element_type=jnp.float32)
    channel_mean = jnp.mean(triangle, axis=0, keepdims=True)
    centered = triangle - channel_mean
    channel_var = jnp.mean(centered * centered, axis=0, keepdims=True)
    return centered / jnp.sqrt(channel_var + EPS)


def dot_nt(a, b):
    return lax.dot_general(a, b, (((1,), (1,)), ((), ())), preferred_element_type=jnp.float32)


def params(limit):
    return pltpu.CompilerParams(vmem_limit_bytes=limit * 1024 * 1024, dimension_semantics=("arbitrary",))


def tiles_kernel(step, scaled, groups, order, inner, *refs):
    if scaled:
        *lefts, right, offset, out, unit = refs
        largest = jnp.zeros(out.shape[1:], jnp.float32)
    else:
        *lefts, right, out = refs
    for c in range(step):
        acc, at = None, 0
        for turn, begins in enumerate(groups):
            one = lefts[at][c]
            for k, begin in enumerate(begins[1:], 1):
                other = inner[0] != 1 if begin is None else pl.program_id(0) >= begin
                one = jnp.where(other, lefts[at + k][c], one)
            at += len(begins)
            term = dot_nt(one, right[order[turn], c])
            acc = term if acc is None else acc + term
        if scaled:
            acc = acc * HALF_SCALE - offset[...]
            largest = jnp.maximum(largest, jnp.abs(acc))
        out[c] = acc

    if scaled:
        here = jnp.full(unit.shape, jnp.max(largest), jnp.float32)

        @pl.when(pl.program_id(0) == 0)
        def _():
            unit[...] = here

        @pl.when(pl.program_id(0) != 0)
        def _():
            unit[...] = jnp.maximum(unit[...], here)

        @pl.when(pl.program_id(0) == pl.num_programs(0) - 1)
        def _():
            unit[...] = jnp.exp2(jnp.ceil(jnp.log2(jnp.maximum(unit[...], 1e-30) * (1.0 / HALF_REACH))))


def tiles(order, inner, lefts, right, right_at, n, offset=None):
    step = 4
    arrays, specs, groups = [], [], []
    rows, depth = lefts[0][0][0].shape[1:]
    cols = right.shape[2]

    def block(index):
        specs.append(pl.BlockSpec((step, rows, depth), lambda c, order, inner: (index(c, inner[0]), 0, 0)))

    for group in lefts:
        if isinstance(group[0], tuple):
            (array, at), *outer = group
            arrays.append(array)
            if not outer:
                block(lambda c, flag, at=at // step: at + c)
            else:
                arrays.append(outer[0][0])
                block(lambda c, flag, at=at // step: at + c * flag)
                block(lambda c, flag, at=outer[0][1] // step: at + c * (1 - flag))
            groups.append((0, None)[: len(group)])
        else:
            begins, begin = [], 0
            for array in group:
                count = array.shape[0] // step
                block(lambda c, flag, begin=begin, count=count: jnp.clip(c - begin, 0, count - 1))
                arrays.append(array)
                begins.append(begin)
                begin += count
            groups.append(tuple(begins))
    specs.append(pl.BlockSpec((4, step, cols, depth), lambda c, *_: (0, right_at // step + c, 0, 0)))
    out_specs = [pl.BlockSpec((step, rows, cols), lambda c, *_: (c, 0, 0))]
    out_shape = [jax.ShapeDtypeStruct((n, rows, cols), jnp.float32)]
    extra = []
    if offset is not None:
        extra.append(offset)
        specs.append(pl.BlockSpec((rows, cols), lambda c, *_: (0, 0)))
        out_specs.append(pl.BlockSpec((8, 128), lambda c, *_: (0, 0)))
        out_shape.append(jax.ShapeDtypeStruct((8, 128), jnp.float32))
    results = pl.pallas_call(
        functools.partial(tiles_kernel, step, offset is not None, tuple(groups)),
        grid_spec=pltpu.PrefetchScalarGridSpec(
            num_scalar_prefetch=2,
            grid=(n // step,),
            in_specs=specs,
            out_specs=out_specs,
        ),
        out_shape=out_shape,
        compiler_params=params(48),
        cost_estimate=pl.CostEstimate(
            flops=8 * n * rows * cols * depth,
            bytes_accessed=n * (4 * (rows + cols) * depth * 2 + rows * cols * 4),
            transcendentals=0,
        ),
        name="tiles",
    )(order, inner, *arrays, right, *extra)
    return results if extra else results[0]


def norm_kernel(both, mine, inner, offset, first, second, *refs):
    *refs, out = refs
    shared, own, sent = refs[:both], refs[both : both + mine], refs[both + mine :]
    share = 1.0 / out.shape[0]

    def write(parts):
        sums, squares = first[...], second[...]
        for part in parts:
            for c in range(part.shape[0]):
                apart = part[c] - offset[...]
                sums += apart
                squares += apart * apart
        shift = sums * share
        channel_var = jnp.maximum(squares * share - shift * shift, 0.0)
        channel_mean = offset[...] + shift
        factor = 1.0 / jnp.sqrt(channel_var + EPS)
        at = 0
        for part in [*shared, *parts]:
            for c in range(part.shape[0]):
                out[at + c] = (part[c] - channel_mean) * factor
            at += part.shape[0]

    @pl.when(inner[0] == 1)
    def _():
        write(own)

    @pl.when(inner[0] != 1)
    def _():
        write(sent)


def norm(inner, stats, shared, own, sent):
    rows, cols = shared[0].shape[1:]
    channels = sum(part.shape[0] for part in [*shared, *own])
    step = 32
    spec = lambda part, used: pl.BlockSpec((part.shape[0], step, cols), lambda i, inner: (0, i * used(inner[0]), 0))
    specs = [pl.BlockSpec((step, cols), lambda i, inner: (i, 0)) for _ in stats]
    specs += [spec(part, lambda flag: 1) for part in shared]
    specs += [spec(part, lambda flag: flag) for part in own]
    specs += [spec(part, lambda flag: 1 - flag) for part in sent]
    size = channels * rows * cols
    return pl.pallas_call(
        functools.partial(norm_kernel, len(shared), len(own)),
        grid_spec=pltpu.PrefetchScalarGridSpec(
            num_scalar_prefetch=1,
            grid=(rows // step,),
            in_specs=specs,
            out_specs=pl.BlockSpec((channels, step, cols), lambda i, inner: (0, i, 0)),
        ),
        out_shape=jax.ShapeDtypeStruct((channels, rows, cols), jnp.float32),
        compiler_params=params(44),
        cost_estimate=pl.CostEstimate(flops=5 * size, bytes_accessed=8 * size, transcendentals=0),
        name="norm",
    )(inner, *stats, *shared, *own, *sent)


SWAP = [(0, 1), (1, 0), (2, 3), (3, 2)]
INWARD = [(0, 1), (3, 2)]
OUTWARD = [(1, 0), (2, 3)]
MIDDLE = [(1, 2), (2, 1)]


def after(block, *done):
    return lax.optimization_barrier((block, *done))[0] if done else block


def line(left, right):
    col = lax.axis_index("col")
    is_inner = (col == 1) | (col == 2)
    inner = is_inner.astype(jnp.int32).reshape(1)
    order = (col ^ jnp.where(is_inner, jnp.array([0, 1, 3, 2], jnp.int32), jnp.array([0, 1, 2, 3], jnp.int32))).astype(jnp.int32)
    unit = left.shape[0] // 16
    near_n, far_n = 8 * unit, 8 * unit
    near_sizes, sizes = [4 * unit, 4 * unit], [2 * unit] * 4

    cut = lambda array, at, n: lax.slice_in_dim(array, at, at + n, axis=0)
    pieces = lambda array, at, counts: [cut(array, at + sum(counts[:k]), n) for k, n in enumerate(counts)]
    go = lambda block, pairs: lax.ppermute(block, "col", pairs)
    rows_of = lambda block: lax.all_gather(block, "row", axis=0, tiled=False)

    right_own = rows_of(right)
    first = cut(left, 0, near_n)
    e_n, p2_n = go(first, SWAP), go(first, MIDDLE)
    left_on = after(left, first)
    second, *split = cut(left_on, near_n, far_n), *pieces(left_on, near_n, [sizes[0], far_n - sizes[0]])
    third = cut(after(right, first), near_n, far_n)
    ended = (e_n, second, *split, third)

    p3_n = go(after(e_n, *ended), MIDDLE)
    r_f = go(after(third, *ended, p2_n), INWARD)
    q2_n = go(after(p2_n, *ended), OUTWARD)
    ended = (p3_n, q2_n)

    right_f = rows_of(after(r_f, *ended))
    p2_f = go(after(second, *ended), MIDDLE)
    e_f = [go(after(split[0], *ended), INWARD)]
    e_f.append(go(after(split[1], *ended, e_f[0]), INWARD))
    q3_na = go(cut(after(p3_n, *ended), 0, near_sizes[0]), OUTWARD)
    q3_nb = go(cut(after(p3_n, *ended, q3_na, right_own), *near_sizes), OUTWARD)

    def near(at, q3, n, *done):
        blocks = [[(after(left, *done), at)], [(e_n, at)], [(p2_n, at), (q2_n, at)], [(p3_n, at), (q3, 0)]]
        return tiles(order, inner, blocks, right_own, at, n)

    def stats_of(offset, block, first, second):
        apart = block - offset
        return first + jnp.sum(apart, axis=0), second + jnp.sum(apart * apart, axis=0)

    near_a = near(0, q3_na, near_sizes[0])
    offset = jnp.mean(near_a, axis=0)
    there = (offset * HALF_SCALE).astype(jnp.float16)
    here = go(there, INWARD)
    stats = stats_of(offset, near_a, 0.0, 0.0)
    p3 = [go(after(e_f[0], there), MIDDLE)]
    ended = (p2_f, *e_f)
    p3 += [go(block, MIDDLE) for block in pieces(after(e_f[1], *ended), 0, sizes[1:])]

    def mine(at, *done):
        e = e_f if at == 0 else [(e_f[1], at - sizes[0])]
        return [[(after(second, *done), at)], e, [(p2_f, at)], p3[: len(p3) // 2] if at == 0 else p3[len(p3) // 2 :]]

    sent, payloads, returned, sizes_out, at = [], [], [], [], 0
    for j, n in enumerate(sizes):
        waits = [*payloads[-1:], *returned[: max(j - 1, 0)], *([near_b] if j == 1 else []), *([q3_nb] if j == 0 else [])]
        blocks = [[(second, at)], [(e_f[1], at - sizes[0]) if j else (e_f[0], 0)], [(p2_f, at)], [(after(p3[j], *waits), 0)]]
        tile, size = tiles(order, inner, blocks, right_f, at, n, here.astype(jnp.float32))
        payload = (tile * (1.0 / size[0, 0])).astype(jnp.float16)
        sizes_out.append(size)
        payloads.append(payload)
        if j == 0:
            near_b = near(near_sizes[0], q3_nb, near_sizes[1], payload)
            stats = stats_of(offset, near_b, *stats)
        ties = [(), (near_b, *returned), (*stats, *returned[1:]), returned[2:]][j]
        if j == len(sizes) - 1:
            own = [tiles(order, inner, mine(0, payloads[-2]), right_own, near_n, far_n // 2)]
            ties = (*ties, *own)
            units = go(jnp.concatenate(sizes_out, axis=0), OUTWARD)
            ties = (*ties, units)
        arrived = go(after(payload, *ties), OUTWARD)
        returned.append(arrived)
        at += n
    for j, arrived in enumerate(returned):
        back = after(arrived, *sent[-1:]).astype(jnp.float32) * units[8 * j, 0]
        sent.append((back + there.astype(jnp.float32)) * (1.0 / HALF_SCALE))
    own.append(tiles(order, inner, mine(far_n // 2, payloads[-1]), right_own, near_n + far_n // 2, far_n // 2))
    return norm(inner, (offset, *stats), [near_a, near_b], own, sent)


def solution(mesh):
    placed = (P("ens", "row", "col"), P("ens", "col", "row"))
    per_device = line if mesh.shape["col"] == 4 and mesh.shape["row"] == 4 else gathered
    return jax.shard_map(
        per_device, mesh=mesh, in_specs=placed, out_specs=P("ens", "row", "col"), check_vma=False
    )
```

```python
import functools

import jax
import jax.numpy as jnp
from jax import lax
from jax.experimental import pallas as pl
from jax.experimental.pallas import tpu as pltpu
from jax.sharding import PartitionSpec as P

EPS = 1e-5
HALF_SCALE = 16.0
HALF_REACH = 32768.0


def gathered(left_proj, right_proj):
    full_left = lax.all_gather(left_proj, "col", axis=2, tiled=True)
    full_right = lax.all_gather(right_proj, "row", axis=2, tiled=True)
    triangle = jnp.einsum("cik,cjk->cij", full_left, full_right, preferred_element_type=jnp.float32)
    channel_mean = jnp.mean(triangle, axis=0, keepdims=True)
    centered = triangle - channel_mean
    channel_var = jnp.mean(centered * centered, axis=0, keepdims=True)
    return centered / jnp.sqrt(channel_var + EPS)


def dot_nt(a, b):
    return lax.dot_general(a, b, (((1,), (1,)), ((), ())), preferred_element_type=jnp.float32)


def params(limit):
    return pltpu.CompilerParams(vmem_limit_bytes=limit * 1024 * 1024, dimension_semantics=("arbitrary",))


def tiles_kernel(step, scaled, groups, order, inner, *refs):
    if scaled:
        *lefts, right, offset, out, unit = refs
        largest = jnp.zeros(out.shape[1:], jnp.float32)
    else:
        *lefts, right, out = refs
    for c in range(step):
        acc, at = None, 0
        for turn, begins in enumerate(groups):
            one = lefts[at][c]
            for k, begin in enumerate(begins[1:], 1):
                other = inner[0] != 1 if begin is None else pl.program_id(0) >= begin
                one = jnp.where(other, lefts[at + k][c], one)
            at += len(begins)
            term = dot_nt(one, right[order[turn], c])
            acc = term if acc is None else acc + term
        if scaled:
            acc = acc * HALF_SCALE - offset[...]
            largest = jnp.maximum(largest, jnp.abs(acc))
        out[c] = acc

    if scaled:
        here = jnp.full(unit.shape, jnp.max(largest), jnp.float32)

        @pl.when(pl.program_id(0) == 0)
        def _():
            unit[...] = here

        @pl.when(pl.program_id(0) != 0)
        def _():
            unit[...] = jnp.maximum(unit[...], here)

        @pl.when(pl.program_id(0) == pl.num_programs(0) - 1)
        def _():
            unit[...] = jnp.exp2(jnp.ceil(jnp.log2(jnp.maximum(unit[...], 1e-30) * (1.0 / HALF_REACH))))


def tiles(order, inner, lefts, right, right_at, n, offset=None):
    step = 4
    arrays, specs, groups = [], [], []
    rows, depth = lefts[0][0][0].shape[1:]
    cols = right.shape[2]

    def block(index):
        specs.append(pl.BlockSpec((step, rows, depth), lambda c, order, inner: (index(c, inner[0]), 0, 0)))

    for group in lefts:
        if isinstance(group[0], tuple):
            (array, at), *outer = group
            arrays.append(array)
            if not outer:
                block(lambda c, flag, at=at // step: at + c)
            else:
                arrays.append(outer[0][0])
                block(lambda c, flag, at=at // step: at + c * flag)
                block(lambda c, flag, at=outer[0][1] // step: at + c * (1 - flag))
            groups.append((0, None)[: len(group)])
        else:
            begins, begin = [], 0
            for array in group:
                count = array.shape[0] // step
                block(lambda c, flag, begin=begin, count=count: jnp.clip(c - begin, 0, count - 1))
                arrays.append(array)
                begins.append(begin)
                begin += count
            groups.append(tuple(begins))
    specs.append(pl.BlockSpec((4, step, cols, depth), lambda c, *_: (0, right_at // step + c, 0, 0)))
    out_specs = [pl.BlockSpec((step, rows, cols), lambda c, *_: (c, 0, 0))]
    out_shape = [jax.ShapeDtypeStruct((n, rows, cols), jnp.float32)]
    extra = []
    if offset is not None:
        extra.append(offset)
        specs.append(pl.BlockSpec((rows, cols), lambda c, *_: (0, 0)))
        out_specs.append(pl.BlockSpec((8, 128), lambda c, *_: (0, 0)))
        out_shape.append(jax.ShapeDtypeStruct((8, 128), jnp.float32))
    results = pl.pallas_call(
        functools.partial(tiles_kernel, step, offset is not None, tuple(groups)),
        grid_spec=pltpu.PrefetchScalarGridSpec(
            num_scalar_prefetch=2,
            grid=(n // step,),
            in_specs=specs,
            out_specs=out_specs,
        ),
        out_shape=out_shape,
        compiler_params=params(48),
        cost_estimate=pl.CostEstimate(
            flops=8 * n * rows * cols * depth,
            bytes_accessed=n * (4 * (rows + cols) * depth * 2 + rows * cols * 4),
            transcendentals=0,
        ),
        name="tiles",
    )(order, inner, *arrays, right, *extra)
    return results if extra else results[0]


def norm_kernel(both, mine, inner, offset, first, second, *refs):
    *refs, out = refs
    shared, own, sent = refs[:both], refs[both : both + mine], refs[both + mine :]
    share = 1.0 / out.shape[0]

    def write(parts):
        sums, squares = first[...], second[...]
        for part in parts:
            for c in range(part.shape[0]):
                apart = part[c] - offset[...]
                sums += apart
                squares += apart * apart
        shift = sums * share
        channel_var = jnp.maximum(squares * share - shift * shift, 0.0)
        channel_mean = offset[...] + shift
        factor = 1.0 / jnp.sqrt(channel_var + EPS)
        at = 0
        for part in [*shared, *parts]:
            for c in range(part.shape[0]):
                out[at + c] = (part[c] - channel_mean) * factor
            at += part.shape[0]

    @pl.when(inner[0] == 1)
    def _():
        write(own)

    @pl.when(inner[0] != 1)
    def _():
        write(sent)


def norm(inner, stats, shared, own, sent):
    rows, cols = shared[0].shape[1:]
    channels = sum(part.shape[0] for part in [*shared, *own])
    step = 32
    spec = lambda part, used: pl.BlockSpec((part.shape[0], step, cols), lambda i, inner: (0, i * used(inner[0]), 0))
    specs = [pl.BlockSpec((step, cols), lambda i, inner: (i, 0)) for _ in stats]
    specs += [spec(part, lambda flag: 1) for part in shared]
    specs += [spec(part, lambda flag: flag) for part in own]
    specs += [spec(part, lambda flag: 1 - flag) for part in sent]
    size = channels * rows * cols
    return pl.pallas_call(
        functools.partial(norm_kernel, len(shared), len(own)),
        grid_spec=pltpu.PrefetchScalarGridSpec(
            num_scalar_prefetch=1,
            grid=(rows // step,),
            in_specs=specs,
            out_specs=pl.BlockSpec((channels, step, cols), lambda i, inner: (0, i, 0)),
        ),
        out_shape=jax.ShapeDtypeStruct((channels, rows, cols), jnp.float32),
        compiler_params=params(26),
        cost_estimate=pl.CostEstimate(flops=5 * size, bytes_accessed=8 * size, transcendentals=0),
        name="norm",
    )(inner, *stats, *shared, *own, *sent)


SWAP = [(0, 1), (1, 0), (2, 3), (3, 2)]
INWARD = [(0, 1), (3, 2)]
OUTWARD = [(1, 0), (2, 3)]
MIDDLE = [(1, 2), (2, 1)]


def after(block, *done):
    return lax.optimization_barrier((block, *done))[0] if done else block


def line(left, right):
    col = lax.axis_index("col")
    is_inner = (col == 1) | (col == 2)
    inner = is_inner.astype(jnp.int32).reshape(1)
    order = (col ^ jnp.where(is_inner, jnp.array([0, 1, 3, 2], jnp.int32), jnp.array([0, 1, 2, 3], jnp.int32))).astype(jnp.int32)
    unit = left.shape[0] // 16
    near_n, far_n = 8 * unit, 8 * unit
    near_sizes, sizes = [4 * unit, 4 * unit], [2 * unit] * 4

    cut = lambda array, at, n: lax.slice_in_dim(array, at, at + n, axis=0)
    pieces = lambda array, at, counts: [cut(array, at + sum(counts[:k]), n) for k, n in enumerate(counts)]
    go = lambda block, pairs: lax.ppermute(block, "col", pairs)
    rows_of = lambda block: lax.all_gather(block, "row", axis=0, tiled=False)

    right_own = rows_of(right)
    first = cut(left, 0, near_n)
    e_n, p2_n = go(first, SWAP), go(first, MIDDLE)
    left_on = after(left, first)
    second, *split = cut(left_on, near_n, far_n), *pieces(left_on, near_n, [sizes[0], far_n - sizes[0]])
    third = cut(after(right, first), near_n, far_n)
    ended = (e_n, second, *split, third)

    p3_n = go(after(e_n, *ended), MIDDLE)
    r_f = go(after(third, *ended, p2_n), INWARD)
    q2_n = go(after(p2_n, *ended), OUTWARD)
    ended = (p3_n, q2_n)

    right_f = rows_of(after(r_f, *ended))
    p2_f = go(after(second, *ended), MIDDLE)
    e_f = [go(after(split[0], *ended), INWARD)]
    e_f.append(go(after(split[1], *ended, e_f[0]), INWARD))
    q3_na = go(cut(after(p3_n, *ended), 0, near_sizes[0]), OUTWARD)
    q3_nb = go(cut(after(p3_n, *ended, q3_na, right_own), *near_sizes), OUTWARD)

    def near(at, q3, n, *done):
        blocks = [[(after(left, *done), at)], [(e_n, at)], [(p2_n, at), (q2_n, at)], [(p3_n, at), (q3, 0)]]
        return tiles(order, inner, blocks, right_own, at, n)

    def stats_of(offset, block, first, second):
        apart = block - offset
        return first + jnp.sum(apart, axis=0), second + jnp.sum(apart * apart, axis=0)

    near_a = near(0, q3_na, near_sizes[0])
    offset = jnp.mean(near_a, axis=0)
    there = (offset * HALF_SCALE).astype(jnp.float16)
    here = go(there, INWARD)
    stats = stats_of(offset, near_a, 0.0, 0.0)
    p3 = [go(after(e_f[0], there), MIDDLE)]
    ended = (p2_f, *e_f)
    p3 += [go(block, MIDDLE) for block in pieces(after(e_f[1], *ended), 0, sizes[1:])]

    def mine(at, *done):
        e = e_f if at == 0 else [(e_f[1], at - sizes[0])]
        return [[(after(second, *done), at)], e, [(p2_f, at)], p3[: len(p3) // 2] if at == 0 else p3[len(p3) // 2 :]]

    sent, payloads, returned, sizes_out, at = [], [], [], [], 0
    for j, n in enumerate(sizes):
        waits = [*payloads[-1:], *returned[: max(j - 1, 0)], *([near_b] if j == 1 else []), *([q3_nb] if j == 0 else [])]
        blocks = [[(second, at)], [(e_f[1], at - sizes[0]) if j else (e_f[0], 0)], [(p2_f, at)], [(after(p3[j], *waits), 0)]]
        tile, size = tiles(order, inner, blocks, right_f, at, n, here.astype(jnp.float32))
        payload = (tile * (1.0 / size[0, 0])).astype(jnp.float16)
        sizes_out.append(size)
        payloads.append(payload)
        if j == 0:
            near_b = near(near_sizes[0], q3_nb, near_sizes[1], payload)
            stats = stats_of(offset, near_b, *stats)
        ties = [(), (near_b, *returned), (*stats, *returned[1:]), returned[2:]][j]
        if j == len(sizes) - 1:
            own = [tiles(order, inner, mine(0, payloads[-2]), right_own, near_n, far_n // 2)]
            ties = (*ties, *own)
            units = go(jnp.concatenate(sizes_out, axis=0), OUTWARD)
            ties = (*ties, units)
        arrived = go(after(payload, *ties), OUTWARD)
        returned.append(arrived)
        at += n
    for j, arrived in enumerate(returned):
        back = after(arrived, *sent[-1:]).astype(jnp.float32) * units[8 * j, 0]
        sent.append((back + there.astype(jnp.float32)) * (1.0 / HALF_SCALE))
    own.append(tiles(order, inner, mine(far_n // 2, payloads[-1]), right_own, near_n + far_n // 2, far_n // 2))
    return norm(inner, (offset, *stats), [near_a, near_b], own, sent)


def solution(mesh):
    placed = (P("ens", "row", "col"), P("ens", "col", "row"))
    per_device = line if mesh.shape["col"] == 4 and mesh.shape["row"] == 4 else gathered
    return jax.shard_map(
        per_device, mesh=mesh, in_specs=placed, out_specs=P("ens", "row", "col"), check_vma=False
    )
```
